32 devices in a mesh: spec: 8 (over z, y), led: 4 (over x, core).
Axes of the slice: x: 2, y: 2, z: 4, core: 2. Of those that a mesh axis runs over, the one named last changes fastest.
Arguments:
- spectrum: float32 [8, 2, 2048, 256], P('spec'), may hold values from -6 to 6
- images: float32 [8, 2, 1024, 1024], P('spec', None, 'led'), may hold values from -6 to 6
- zernike: float32 [8, 16], P('spec'), may hold values from -6 to 6
- pupil_modes: float32 [16, 4, 31], P('led'), may hold values from -0.1875 to 0.1875
- patch_tiles: int32 [8, 25], replicated, may hold values from 0 to 63, as said below
- patch_offsets: int32 [8, 2], replicated, may hold values from 0 to 226
Outputs:
- new_spectrum: float32 [8, 2, 2048, 256], P('spec')
- solve_residual: float32 [8, 2, 2048, 256], P('spec')
The draws below stay inside these ranges and needn't reach their ends.
Inputs may be any that keep to these rules, and one draw needn't show every extreme that they name: Row l of patch_tiles lists the ids (r + i) * 8 + c + j of a block of 5 x 5 tiles with top left tile (r, c), i and j from 0 to 4, row by row.
All inputs are finite; a program needn't handle non-finite values.
Results may differ from the reference program's by a relative error of at most 0.0003.
Values sent between devices are 32-bit elements; how exact they have to be, the bound alone decides.
A program may use at most 192 MiB of HBM per device.

```python
import jax
import jax.numpy as jnp
from jax import lax

TILE = 256
WIN = 5
TAPS = 31
CHANNELS = 16
IMG = 1024
ITERS = 1
ROWS = 8
COLS = 8
LEDS = 8


def draw_patch_tiles(key, part):
    key_rows, key_cols = jax.random.split(key, 2)
    top_rows = jax.random.randint(key_rows, (LEDS,), 0, ROWS - WIN + 1).astype(jnp.int32)
    left_cols = jax.random.randint(key_cols, (LEDS,), 0, COLS - WIN + 1).astype(jnp.int32)
    top_rows = top_rows.at[0].set(0).at[LEDS - 1].set(ROWS - WIN)
    left_cols = left_cols.at[0].set(0).at[LEDS - 1].set(COLS - WIN)
    row_steps = jnp.arange(WIN, dtype=jnp.int32)[:, None]
    col_steps = jnp.arange(WIN, dtype=jnp.int32)[None, :]
    tile_ids = (top_rows[:, None, None] + row_steps) * COLS + left_cols[:, None, None] + col_steps
    return tile_ids.reshape(LEDS, WIN * WIN).astype(jnp.int32)


def place_ends(result, own_key, low, largest):
    place = [jax.random.randint(jax.random.fold_in(own_key, axis), (), 0, length) for axis, length in enumerate(result.shape)]
    widest = result.shape.index(max(result.shape))
    next_to = place[:widest] + [(place[widest] + 1) % result.shape[widest]] + place[widest + 1:]
    return result.at[tuple(place)].set(low).at[tuple(next_to)].set(largest)


def steps_of(stream_key, shape, pieces, least, largest):
    gain = 1.0
    for position, blocks in pieces:
        heights = jax.random.uniform(jax.random.fold_in(jax.random.fold_in(stream_key, 6), position), (blocks,), jnp.float32, least / len(pieces), largest / len(pieces))
        gain = gain * jnp.repeat(jnp.exp(heights), shape[position] // blocks).reshape((-1,) + (1,) * (len(shape) - 1 - position))
    return gain


def scatter_about(rng, extent, scale, reach, shards=(), held_as=jnp.bfloat16):
    result = jax.random.normal(rng, extent, jnp.float32) * scale
    if len(shards) > 0:
        result = steps_of(rng, extent, shards, -0.22, 0.18) * result
    return jnp.clip(result, min=-reach, max=reach).astype(held_as)


def setup_inputs(seed: int = 0) -> dict:
    key_list = jax.random.split(jax.random.key(seed), 7)
    spectrum = scatter_about(key_list[0], (COLS, 2, ROWS * TILE, TILE), 1.0, 6.0, ((0, 8),), jnp.float32)
    images = scatter_about(key_list[1], (LEDS, 2, IMG, IMG), 1.0, 6.0, ((0, 8), (2, 4)), jnp.float32)
    zernike = scatter_about(key_list[2], (LEDS, CHANNELS), 1.0, 6.0, ((0, 8),), jnp.float32)
    pupil_modes = scatter_about(key_list[3], (CHANNELS, 4, TAPS), (2 * CHANNELS * TAPS) ** -0.5, 0.1875, ((0, 4),), jnp.float32)
    patch_tiles = draw_patch_tiles(jax.random.fold_in(key_list[6], 71), 0)
    patch_offsets = place_ends(jax.random.randint(key_list[5], (LEDS, 2), 0, WIN * TILE - IMG - TAPS + 2), jax.random.fold_in(key_list[5], 1), 0, (WIN * TILE - IMG - TAPS + 2) - 1).astype(jnp.int32)
    return dict(spectrum=spectrum, images=images, zernike=zernike, pupil_modes=pupil_modes, patch_tiles=patch_tiles, patch_offsets=patch_offsets)


damping = 0.5


def toeplitz(kernel, offset, rows_len, cols_len):
    tap_count = kernel.shape[-1]
    distance = jnp.arange(rows_len, dtype=jnp.int32)[:, None] - offset - jnp.arange(cols_len, dtype=jnp.int32)[None, :]
    matrix = jnp.zeros((2, rows_len, cols_len), kernel.dtype)
    for tap in range(tap_count):
        matrix = matrix + jnp.where(distance[None, :, :] == tap, kernel[:, tap][:, None, None], jnp.zeros((), kernel.dtype))
    return matrix


def complex_product(left_side, right_side):
    real_part = jnp.dot(left_side[0], right_side[0], precision=lax.Precision.HIGHEST) - jnp.dot(left_side[1], right_side[1], precision=lax.Precision.HIGHEST)
    imag_part = jnp.dot(left_side[0], right_side[1], precision=lax.Precision.HIGHEST) + jnp.dot(left_side[1], right_side[0], precision=lax.Precision.HIGHEST)
    return jnp.stack([real_part, imag_part])


def plain_swap(matrix):
    return jnp.stack([matrix[0].T, matrix[1].T])


def conj_swap(matrix):
    return jnp.stack([matrix[0].T, -matrix[1].T])


def conjugate(matrix):
    return jnp.stack([matrix[0], -matrix[1]])


def forward_cols(window, col_map):
    return complex_product(window, col_map)


def forward_rows(columns, row_map):
    return complex_product(plain_swap(row_map), columns)


def adjoint_rows(picture, row_map):
    return complex_product(conjugate(row_map), picture)


def adjoint_cols(columns, col_map):
    return complex_product(columns, conj_swap(col_map))


def reference(spectrum, images, zernike, pupil_modes, patch_tiles, patch_offsets):
    block_len = WIN * TILE
    row_cells = ROWS * TILE
    anchor = jnp.int32(0)
    kernels = jnp.dot(zernike, pupil_modes.reshape(CHANNELS, 4 * TAPS), precision=lax.Precision.HIGHEST).reshape(LEDS, 4, TAPS)

    def to_grid(tiles):
        return tiles.transpose(1, 2, 0, 3).reshape(2, row_cells, COLS * TILE)

    def to_tiles(grid):
        return grid.reshape(2, row_cells, COLS, TILE).transpose(2, 0, 1, 3)

    def normal_sweep(source_tiles, with_data):
        source_grid = to_grid(source_tiles)

        def advance(accumulated, member):
            first_tile, offsets, kernel, picture = member
            top_row = (first_tile // COLS) * TILE
            left_col = (first_tile % COLS) * TILE
            col_map = toeplitz(kernel[0:2], offsets[1], block_len, IMG)
            row_map = toeplitz(kernel[2:4], offsets[0], block_len, IMG)
            window = lax.dynamic_slice(source_grid, (anchor, top_row, left_col), (2, block_len, block_len))
            modelled = forward_rows(forward_cols(window, col_map), row_map)
            misfit = picture - modelled if with_data else modelled
            returned = adjoint_cols(adjoint_rows(misfit, row_map), col_map)
            current = lax.dynamic_slice(accumulated, (anchor, top_row, left_col), (2, block_len, block_len))
            return lax.dynamic_update_slice(accumulated, current + returned, (anchor, top_row, left_col)), None

        total = lax.scan(advance, jnp.zeros_like(source_grid), (patch_tiles[:, 0], patch_offsets, kernels, images))[0]
        return to_tiles(total)

    residual = normal_sweep(spectrum, True) - damping * spectrum
    direction = residual
    update = jnp.zeros_like(residual)
    norm_now = jnp.sum(residual * residual)
    for iteration in range(ITERS):
        image_dir = normal_sweep(direction, False) + damping * direction
        step_size = norm_now / jnp.sum(direction * image_dir)
        update = update + step_size * direction
        residual = residual - step_size * image_dir
        norm_next = jnp.sum(residual * residual)
        direction = residual + (norm_next / norm_now) * direction
        norm_now = norm_next
    return spectrum + update, residual
```

```python
import functools

import jax
import jax.numpy as jnp
import numpy as np
from jax import lax
from jax.experimental import pallas as pl
from jax.experimental.pallas import tpu as pltpu
from jax.sharding import PartitionSpec as P

WIN = 5
damping = 0.5
HALO = 64
EDGE = 32
STEP = 192
SPAN = 256
HIGHEST = lax.Precision.HIGHEST


def params(mib, **kw):
    return pltpu.CompilerParams(vmem_limit_bytes=mib * 2**20, **kw)


def split(x):
    high = x.astype(jnp.bfloat16)
    return high, (x - high.astype(jnp.float32)).astype(jnp.bfloat16)


def mm(a, b):
    return jnp.dot(a, b, preferred_element_type=jnp.float32)


def mm3(a_high, a_low, b_high, b_low):
    return mm(a_high, b_high) + mm(a_high, b_low) + mm(a_low, b_high)


def skew(table, shift, width):
    rows, lanes = table.shape
    if width > lanes:
        table = jnp.concatenate([table, jnp.zeros((rows, width - lanes), table.dtype)], axis=1)
    return pltpu.roll(table, shift % width, 1, stride=1, stride_axis=0)


def place_kernel(shift_ref, image_ref, out_ref):
    rows, lanes = image_ref.shape
    slots, _, tile = out_ref.shape
    wide = jnp.concatenate([image_ref[...], jnp.zeros((rows, slots * tile - lanes), jnp.float32)], axis=1)
    wide = pltpu.roll(wide, shift_ref[0], 1)
    for slot in range(slots):
        out_ref[slot] = wide[:, slot * tile : (slot + 1) * tile]


def place(image, shift, slots, tile):
    rows, lanes = image.shape
    step = 64
    return pl.pallas_call(
        place_kernel,
        out_shape=jax.ShapeDtypeStruct((slots, rows, tile), jnp.float32),
        grid_spec=pltpu.PrefetchScalarGridSpec(
            num_scalar_prefetch=1,
            grid=(rows // step,),
            in_specs=[pl.BlockSpec((step, lanes), lambda i, s: (i, 0))],
            out_specs=pl.BlockSpec((slots, step, tile), lambda i, s: (0, i, 0)),
        ),
        compiler_params=params(32),
        name="place",
    )(shift, image)


def back_kernel(base_ref, taps_ref, got_ref, out_ref, acc):
    led = pl.program_id(0)
    _, strip2, tile = got_ref.shape
    strip = strip2 // 2
    quarters, ext, width = out_ref.shape
    own = ext - 2 * EDGE
    tall = strip + 48

    @pl.when(led == 0)
    def _():
        acc[...] = jnp.zeros_like(acc)

    taps = taps_ref[0]
    col = [skew(jnp.broadcast_to(taps[p : p + 1], (tile, 2 * tile)), 0, 2 * tile) for p in (0, 1)]
    cr, ci = col[0], -col[1]
    crm, cim = cr[:, :tile], ci[:, :tile]
    crs, cis = cr[:, tile : tile + HALO], ci[:, tile : tile + HALO]
    top = jnp.concatenate([crm, cim, crs, cis], axis=1)
    low = jnp.concatenate([-cim, crm, -cis, crs], axis=1)
    t_high, t_low = split(jnp.concatenate([top, low], axis=0))
    got = got_ref[0]
    g_high, g_low = split(jnp.concatenate([got[:strip], got[strip:]], axis=1))
    u = mm3(g_high, g_low, t_high, t_low)
    spill = u[:, 2 * tile :]
    lane = lax.broadcasted_iota(jnp.int32, spill.shape, 1)
    turned = pltpu.roll(spill, HALO, 1) * jnp.where(lane < HALO, -1.0, 1.0)
    v = jnp.concatenate([-u[:, tile : 2 * tile], u[:, :tile], turned], axis=1)
    u_high, u_low = split(jnp.concatenate([u, v], axis=0))
    row = [skew(jnp.broadcast_to(taps[p : p + 1, : 2 * strip], (tall, 2 * strip)), -EDGE - 8, 2 * strip)[:, :strip] for p in (2, 3)]
    r_high, r_low = split(jnp.concatenate([row[0], -row[1]], axis=1))
    piece = mm3(r_high, r_low, u_high, u_low)
    base = pl.multiple_of(base_ref[led], 8)
    acc[pl.ds(base, tall), :] += piece

    @pl.when(led == pl.num_programs(0) - 1)
    def _():
        for q in range(quarters):
            out_ref[q] = acc[q * own : q * own + ext, :]


def backproject(got, taps, base, quarters, row_cells):
    leds, strip2, tile = got.shape
    own = row_cells // quarters
    width = 2 * tile + 2 * HALO
    return pl.pallas_call(
        back_kernel,
        out_shape=jax.ShapeDtypeStruct((quarters, own + 2 * EDGE, width), jnp.float32),
        grid_spec=pltpu.PrefetchScalarGridSpec(
            num_scalar_prefetch=1,
            grid=(leds,),
            in_specs=[
                pl.BlockSpec((1, 8, taps.shape[2]), lambda i, s: (i, 0, 0)),
                pl.BlockSpec((1, strip2, tile), lambda i, s: (i, 0, 0)),
            ],
            out_specs=pl.BlockSpec((quarters, own + 2 * EDGE, width), lambda i, s: (0, 0, 0)),
            scratch_shapes=[pltpu.VMEM((row_cells + 2 * EDGE, width), jnp.float32)],
        ),
        compiler_params=params(40),
        name="backproject",
    )(base, taps, got)


def normal_kernel(lead, field_ref, col_ref, row_ref, out_ref, f_high, f_low, u_high, u_low):
    led = pl.program_id(0)
    rows_in, _ = field_ref.shape
    rows_out, wide = out_ref.shape
    tile = wide // 2

    @pl.when(led == 0)
    def _():
        high, low = split(field_ref[...])
        f_high[...] = high
        f_low[...] = low
        out_ref[...] = damping * field_ref[EDGE : EDGE + rows_out, :wide]

    parts = []
    for p in (0, 1):
        table = col_ref[0, p]
        main = skew(table[:tile], -EDGE, 2 * tile)[:, :tile]
        left = skew(table[tile : tile + HALO], -HALO - EDGE, 2 * tile)[:, :tile]
        right = skew(table[tile + HALO :], tile - EDGE, 2 * tile)[:, :tile]
        parts.append((main, jnp.concatenate([left, right], axis=0)))
    (rm, rh), (im, ih) = parts
    matrix = jnp.concatenate(
        [
            jnp.concatenate([rm, im], axis=1),
            jnp.concatenate([-im, rm], axis=1),
            jnp.concatenate([rh, ih], axis=1),
            jnp.concatenate([-ih, rh], axis=1),
        ],
        axis=0,
    )
    m_high, m_low = split(matrix)
    chunk = rows_in // 2
    for k in range(2):
        rows = slice(k * chunk, (k + 1) * chunk)
        u = mm3(f_high[rows, :], f_low[rows, :], m_high, m_low)
        high, low = split(u)
        u_high[rows, :] = high
        u_low[rows, :] = low

    def both(ref, start, size):
        u = ref[start : start + size, :]
        v = jnp.concatenate([-u[:, tile:], u[:, :tile]], axis=1)
        if size < SPAN:
            pad = jnp.zeros((SPAN - size, 2 * tile), u.dtype)
            return jnp.concatenate([u, pad, v, pad], axis=0)
        return jnp.concatenate([u, v], axis=0)

    for start in range(0, rows_out, STEP):
        count = min(STEP, rows_out - start)
        size = min(SPAN, rows_in - start)
        sel = slice(lead + start, lead + start + count)
        pr = skew(row_ref[0, 0, sel, :], 0, SPAN)
        pi = skew(row_ref[0, 1, sel, :], 0, SPAN)
        p_high, p_low = split(jnp.concatenate([pr, -pi], axis=1))
        out_ref[start : start + count, :] += mm3(
            p_high, p_low, both(u_high, start, size), both(u_low, start, size)
        )


def normal(field, col_table, row_table, lead, rows_out):
    rows_in, wide = field.shape
    tile = wide // 3
    leds = col_table.shape[0]
    return pl.pallas_call(
        functools.partial(normal_kernel, lead),
        out_shape=jax.ShapeDtypeStruct((rows_out, 2 * tile), jnp.float32),
        grid=(leds,),
        in_specs=[
            pl.BlockSpec(field.shape, lambda i: (0, 0)),
            pl.BlockSpec((1,) + col_table.shape[1:], lambda i: (i, 0, 0, 0)),
            pl.BlockSpec((1,) + row_table.shape[1:], lambda i: (i, 0, 0, 0)),
        ],
        out_specs=pl.BlockSpec((rows_out, 2 * tile), lambda i: (0, 0)),
        scratch_shapes=[
            pltpu.VMEM((rows_in, wide), jnp.bfloat16),
            pltpu.VMEM((rows_in, wide), jnp.bfloat16),
            pltpu.VMEM((rows_in, 2 * tile), jnp.bfloat16),
            pltpu.VMEM((rows_in, 2 * tile), jnp.bfloat16),
        ],
        compiler_params=params(48),
        name="normal",
        cost_estimate=pl.CostEstimate(
            flops=leds * 2 * 3 * (rows_in * 768 * 512 + rows_out * 512 * 512),
            bytes_accessed=12 * 2**20,
            transcendentals=0,
        ),
    )(field, col_table, row_table)


def body(spectrum, images, zernike, pupil_modes, patch_tiles, patch_offsets):
    tile = spectrum.shape[3]
    row_cells = spectrum.shape[2]
    strip = images.shape[2]
    image_len = images.shape[3]
    channels = zernike.shape[1]
    tap_count = pupil_modes.shape[2]
    reach = tap_count - 1
    spec_count = lax.axis_size("spec")
    led_count = lax.axis_size("led")
    column = lax.axis_index("spec")
    quarter = lax.axis_index("led")
    own = row_cells // led_count
    ext = own + 2 * EDGE

    tops = (patch_tiles[:, 0] // spec_count) * tile + patch_offsets[:, 0]
    lefts = (patch_tiles[:, 0] % spec_count) * tile + patch_offsets[:, 1]

    own_left = lax.dynamic_slice_in_dim(lefts, column, 1)
    slots = place(images.reshape(2 * strip, image_len), own_left, spec_count, tile)
    got = lax.all_to_all(slots, "spec", split_axis=0, concat_axis=0, tiled=True)

    modes = lax.all_gather(pupil_modes, "led", axis=0, tiled=True).reshape(channels, 4 * tap_count)
    coeffs = lax.all_gather(zernike, "spec", axis=0, tiled=True)
    kernels = jnp.dot(coeffs, modes, precision=HIGHEST).reshape(spec_count, 4, tap_count)

    spread = np.zeros((tap_count, tap_count, 128), np.float32)
    for tap in range(tap_count):
        for m in range(2 * tap_count - 1):
            other = tap + m - reach
            if 0 <= other < tap_count:
                spread[other, tap, m + EDGE - reach] = 1.0
    shifted = jnp.einsum("lqo,otm->lqtm", kernels, jnp.asarray(spread), precision=HIGHEST)

    def products(re, im):
        kr, ki = kernels[:, re, :, None], kernels[:, im, :, None]
        sr, si = shifted[:, re], shifted[:, im]
        return jnp.stack([kr * sr + ki * si, ki * sr - kr * si], axis=1)

    def band(cells, starts, prods):
        tap = jnp.arange(tap_count, dtype=jnp.int32)[None, None, :]
        gap = cells[None, :, None] - starts[:, None, None]
        inside = ((tap <= gap) & (tap > gap - image_len)).astype(jnp.float32)
        return jnp.einsum("lxt,lptm->lpxm", inside, prods, precision=HIGHEST)

    col_cells = column * tile + jnp.concatenate(
        [
            jnp.arange(tile, dtype=jnp.int32),
            jnp.arange(-HALO, 0, dtype=jnp.int32),
            jnp.arange(tile, tile + HALO, dtype=jnp.int32),
        ]
    )
    row_cells_here = quarter * own - EDGE + jnp.arange(ext, dtype=jnp.int32)
    col_table = band(col_cells, lefts, products(0, 1))
    row_table = band(row_cells_here, tops, products(2, 3))

    first = tops + quarter * strip + EDGE
    base = first // 8 * 8
    lane = jnp.arange(2 * tile, dtype=jnp.int32)[None, None, :]
    tap = jnp.arange(tap_count, dtype=jnp.int32)[None, :, None]
    late = EDGE + 8 - (first - base)
    backward = (lane == late[:, None, None] - tap).astype(jnp.float32)
    back = jnp.einsum("lpt,ltj->lpj", kernels[:, 2:4], backward, precision=HIGHEST)
    onward = jnp.pad(kernels[:, 0:2], ((0, 0), (0, 0), (0, 2 * tile - tap_count)))
    taps = jnp.pad(jnp.concatenate([onward, back], axis=1), ((0, 0), (0, 4), (0, 0)))

    to_right = [(i, i + 1) for i in range(spec_count - 1)]
    to_left = [(i + 1, i) for i in range(spec_count - 1)]

    def pack(parts):
        return jnp.concatenate([parts[0], parts[1]], axis=1)

    padded = jnp.pad(spectrum[0], ((0, 0), (2 * EDGE, 2 * EDGE), (0, 0)))
    here = lax.dynamic_slice_in_dim(padded, quarter * own, own + 4 * EDGE, 1)
    from_left = lax.ppermute(here[:, :, tile - HALO :], "spec", to_right)
    from_right = lax.ppermute(here[:, :, :HALO], "spec", to_left)
    field = jnp.concatenate(
        [here[0], here[1], from_left[0], from_right[0], from_left[1], from_right[1]], axis=1
    )
    modelled = normal(field, col_table, row_table, 0, ext)

    partial = backproject(got, taps, base, led_count, row_cells)
    summed = lax.psum_scatter(partial, "led", scatter_dimension=0, tiled=False)

    rough = summed[:, : 2 * tile] - modelled
    spill = summed[:, 2 * tile :]
    rr, ri = rough[:, :tile], rough[:, tile:]
    rightward = jnp.concatenate([rr[:, tile - HALO :], ri[:, tile - HALO :], spill], axis=1)
    leftward = jnp.concatenate([rr[:, :HALO], ri[:, :HALO]], axis=1)
    left_in = lax.ppermute(rightward, "spec", to_right)
    right_in = lax.ppermute(leftward, "spec", to_left) + spill
    spill_in = left_in[:, 2 * HALO :]
    start_r = rr[:, :HALO] + spill_in[:, :HALO]
    start_i = ri[:, :HALO] + spill_in[:, HALO:]
    residual_ext = jnp.concatenate(
        [
            start_r,
            rr[:, HALO:],
            start_i,
            ri[:, HALO:],
            left_in[:, :HALO],
            right_in[:, :HALO],
            left_in[:, HALO : 2 * HALO],
            right_in[:, HALO:],
        ],
        axis=1,
    )
    residual_own = residual_ext[EDGE : EDGE + own, : 2 * tile]
    residual_all = lax.all_gather(residual_own, "led", axis=0, tiled=True)
    image_own = normal(residual_ext, col_table, row_table, EDGE, own)
    sums = jnp.stack([jnp.sum(residual_own * residual_own), jnp.sum(residual_own * image_own)])
    totals = lax.psum(sums, ("spec", "led"))
    image_all = lax.all_gather(image_own, "led", axis=0, tiled=True)
    step_size = totals[0] / totals[1]

    def unpack(packed):
        return jnp.stack([packed[:, :tile], packed[:, tile:]])

    final = unpack(residual_all)
    return (
        (spectrum[0] + step_size * final)[None],
        (final - step_size * unpack(image_all))[None],
    )


def solution(mesh):
    placed = (
        P("spec", None, None, None),
        P("spec", None, "led", None),
        P("spec", None),
        P("led", None, None),
        P(),
        P(),
    )
    return jax.shard_map(
        body,
        mesh=mesh,
        in_specs=placed,
        out_specs=(P("spec", None, None, None), P("spec", None, None, None)),
        check_vma=False,
    )
```
